1024 devices in a mesh: dp: 64 (over x, z), expert: 16 (over y, core).
Axes of the slice: x: 4, y: 8, z: 16, core: 2. Of those that a mesh axis runs over, the one named last changes fastest.
Arguments:
- out_grad: bfloat16 [131072, 1440], P(('dp', 'expert')), may hold values from -0.022094727 to 0.022094727
- routes: int32 [131072, 4], P(('dp', 'expert')), may hold values from 0 to 3, as said below
- slots: int32 [131072, 4], P(('dp', 'expert')), may hold values from 0 to 127, as said below
- combine_weight: bfloat16 [131072, 4], P(('dp', 'expert')), may hold values from 0.049804688 to 1
- saved_hidden: bfloat16 [64, 16, 16, 128, 360], P('dp', 'expert'), may hold values from -6 to 6
- saved_out: bfloat16 [64, 16, 16, 128, 360], P('dp', 'expert'), may hold values from -12 to 12
Outputs:
- weight_grad: bfloat16 [16, 518400], P('expert', 'dp')
- router_grad: float32 [131072, 4], P(('dp', 'expert'))
The draws below stay inside these ranges and needn't reach their ends.
Inputs may be any that keep to these rules, and one draw needn't show every extreme that they name: Each token names 4 different experts; the routes of one device name each expert at most 128 times and some expert exactly 128 times. The routes of one device to one expert hold distinct slots, from 0 up to their number minus one.
All inputs are finite; a program needn't handle non-finite values.
Results may differ from the reference program's by a relative error of at most 0.0049.
Values may be sent and summed in bfloat16 or wider, within the bound.
No kernel may reach another device: no remote copies, remote signals or barrier semaphores. Data moves between devices by JAX's collectives and lax.ppermute only.
A program may use at most 64 MiB of HBM per device.

```python
import jax
import jax.numpy as jnp
from jax import lax

D = 1440
FF = 1440
TOPK = 4
TOK_DEV = 128
EXPERTS = 4
SPLIT = 4
TOKENS = 131072
CAP = 128
N_DP = 64
N_EXPERT = 16


def route_table(key):
    blocks = TOKENS // TOK_DEV
    route_total = 4 * TOK_DEV
    even_share = route_total // EXPERTS
    headroom = CAP - even_share
    key_busy, key_short, key_pick, key_token, key_column, key_cell = jax.random.split(key, 6)
    expert_ids = jnp.arange(EXPERTS, dtype=jnp.int32)[None, :]
    busiest = jax.random.randint(key_busy, (blocks, 1), 0, EXPERTS).astype(jnp.int32)
    shorted = (busiest + 1 + jax.random.randint(key_short, (blocks, headroom), 0, EXPERTS - 1)) % EXPERTS
    deficit = jnp.sum((shorted[:, :, None] == expert_ids[:, None, :]).astype(jnp.int32), axis=1)
    counts = even_share + headroom * (expert_ids == busiest).astype(jnp.int32) - deficit
    counts = counts.astype(jnp.int32)
    jitter = jax.random.randint(key_pick, (TOK_DEV, blocks, EXPERTS), 0, 256).astype(jnp.int32)
    tokens_left = (TOK_DEV - jnp.arange(TOK_DEV, dtype=jnp.int32)).astype(jnp.int32)

    def choose(remain, inputs):
        left_now, jitter_row = inputs
        forced = (remain >= left_now).astype(jnp.int32)
        positive = (remain > 0).astype(jnp.int32)
        scores = forced * 536870912 + positive * 268435456 + jitter_row * remain * EXPERTS + expert_ids
        picked = lax.top_k(scores, 4)[1].astype(jnp.int32)
        taken = jnp.sum((picked[:, :, None] == expert_ids[:, None, :]).astype(jnp.int32), axis=1)
        return (remain - taken, picked)
    final_left, chosen = lax.scan(choose, counts, (tokens_left, jitter))
    chosen = chosen.transpose(1, 0, 2)
    token_orders = jax.vmap(lambda single: jax.random.permutation(single, TOK_DEV))(jax.random.split(key_token, blocks))
    chosen = jnp.take_along_axis(chosen, token_orders.astype(jnp.int32)[:, :, None], axis=1)
    column_keys = jax.random.randint(key_column, (blocks, TOK_DEV, 4), 0, 1024) * 4 + jnp.arange(4, dtype=jnp.int32)[None, None, :]
    column_order = jnp.argsort(column_keys, axis=-1).astype(jnp.int32)
    chosen = jnp.take_along_axis(chosen, column_order, axis=-1)
    flat = chosen.reshape(blocks, route_total)
    shuffle_keys = jax.vmap(lambda single: jax.random.permutation(single, route_total))(jax.random.split(key_cell, blocks))
    sort_key = flat * route_total + shuffle_keys.astype(jnp.int32)
    order = jnp.argsort(sort_key, axis=1).astype(jnp.int32)
    position = jnp.argsort(order, axis=1).astype(jnp.int32)
    starts = jnp.cumsum(counts, axis=1) - counts
    cell_start = jnp.take_along_axis(starts, flat, axis=1)
    slot_ids = position - cell_start
    return (flat.reshape(TOKENS, 4).astype(jnp.int32), slot_ids.reshape(TOKENS, 4).astype(jnp.int32))


def draw_routes(key, part):
    return route_table(key)[0]


def draw_slots(key, part):
    return route_table(key)[1]


def spiked(entries, own_key, source, target, shards_of, factor):
    def block_of(dim):
        return (jnp.arange(entries.shape[dim]) // (entries.shape[dim] // shards_of)).reshape((-1,) + (1,) * (entries.ndim - 1 - dim))

    near = jax.random.permutation(own_key, shards_of)[block_of(target)]
    far = (block_of(target) + shards_of // 2) % shards_of
    return jnp.where((block_of(source) == near) | (block_of(source) == far), factor * entries, entries)


def block_levels(stream_key, extent, cuts, low, largest):
    gain = 1.0
    for dim, blocks in cuts:
        heights = jax.random.uniform(jax.random.fold_in(jax.random.fold_in(stream_key, 6), dim), (blocks,), jnp.float32, low / len(cuts), largest / len(cuts))
        gain = gain * jnp.repeat(jnp.exp(heights), extent[dim] // blocks).reshape((-1,) + (1,) * (len(extent) - 1 - dim))
    return gain


def noise(own_key, shape, deviation, reach, cuts=(), kind=jnp.bfloat16):
    factor_of = block_levels(own_key, shape, cuts, -0.22, 0.18) if cuts else 1.0
    result = jax.random.normal(own_key, shape, jnp.float32) * deviation * factor_of
    return jnp.minimum(jnp.maximum(result, -reach), reach).astype(kind)


def noise_with(key, shape, width, most, pieces, heavy, kind=jnp.bfloat16):
    drawn = width * jax.random.normal(key, shape, jnp.float32)
    if pieces:
        drawn = drawn * block_levels(key, shape, pieces, -0.22, 0.18)
    return jnp.clip(spiked(drawn, jax.random.fold_in(key, 3), *heavy), -most, most).astype(kind)


def setup_inputs(seed: int = 0) -> dict:
    key_list = jax.random.split(jax.random.key(seed), 7)
    return {
        "out_grad": noise(key_list[0], (TOKENS, D), (2 * (4 * TOKENS // EXPERTS) ** -0.5), 0.022094727, ((0, 1024),)),
        "routes": draw_routes(jax.random.fold_in(key_list[6], 71), 0),
        "slots": draw_slots(jax.random.fold_in(key_list[6], 71), 0),
        "combine_weight": jnp.clip(0.049804688 + 0.9501953 * jax.random.uniform(key_list[3], (TOKENS, TOPK), jnp.float32) ** block_levels(key_list[3], (TOKENS, TOPK), ((0, 1024),), -0.2, 0.2), 0.049804688, 1.0).astype(jnp.bfloat16),
        "saved_hidden": noise_with(key_list[4], (N_DP, N_EXPERT, N_EXPERT, CAP, FF // SPLIT), 1.0, 6.0, ((0, 64), (1, 16)), (0, 4, 8, 2.0)),
        "saved_out": noise(key_list[5], (N_DP, N_EXPERT, N_EXPERT, CAP, D // SPLIT), 2.0, 12.0, ((0, 64), (1, 16))),
    }


def reference(out_grad, routes, slots, combine_weight, saved_hidden, saved_out):
    blocks_all = saved_hidden.shape[1]
    sources = saved_hidden.shape[2]
    capacity = saved_hidden.shape[3]
    hidden_units = saved_hidden.shape[4]
    feature_count = out_grad.shape[1]
    part_width = saved_out.shape[4]
    split_count = blocks_all // EXPERTS
    grad_rows = out_grad.reshape(N_DP, sources, TOK_DEV, feature_count)
    route_rows = routes.reshape(N_DP, sources, TOK_DEV, TOPK).astype(jnp.int32)
    slot_rows = slots.reshape(N_DP, sources, TOK_DEV, TOPK).astype(jnp.int32)
    weight_rows = combine_weight.reshape(N_DP, sources, TOK_DEV, TOPK)
    source_ids = jnp.broadcast_to(jnp.arange(sources, dtype=jnp.int32)[:, None, None], (sources, TOK_DEV, TOPK))

    def row_step(total, inputs):
        grad_row, route_row, slot_row, weight_row, hidden_row, out_row = inputs
        spread = jnp.broadcast_to(grad_row[:, :, None, :], (sources, TOK_DEV, TOPK, feature_count))
        received = jnp.zeros((EXPERTS, sources, capacity, feature_count), jnp.bfloat16)
        received = received.at[route_row, source_ids, slot_row].set(spread)
        weights = jnp.zeros((EXPERTS, sources, capacity), jnp.bfloat16)
        weights = weights.at[route_row, source_ids, slot_row].set(weight_row)
        out_full = out_row.reshape(EXPERTS, split_count, sources, capacity, part_width)
        out_full = out_full.transpose(0, 2, 3, 1, 4).reshape(EXPERTS, sources, capacity, feature_count)
        picked = out_full[route_row, source_ids, slot_row]
        scores = jnp.sum(picked.astype(jnp.float32) * spread.astype(jnp.float32), axis=-1)
        scaled = (weights.astype(jnp.float32)[..., None] * received.astype(jnp.float32)).astype(jnp.bfloat16)
        scaled_blocks = jnp.repeat(scaled, split_count, axis=0)
        partial_sum = jnp.einsum("isrf,isrd->ifd", hidden_row.astype(jnp.float32), scaled_blocks.astype(jnp.float32),
                                 precision=lax.Precision.HIGHEST)
        return total + partial_sum, scores

    start_total = jnp.zeros((blocks_all, hidden_units, feature_count), jnp.float32)
    total, scores = lax.scan(row_step, start_total, (grad_rows, route_rows, slot_rows, weight_rows, saved_hidden, saved_out))
    flat_total = total.reshape(blocks_all, hidden_units * feature_count)
    return (flat_total.astype(jnp.bfloat16), scores.reshape(TOKENS, TOPK))
```

```python
import jax
import jax.numpy as jnp
from jax import lax
from jax.experimental import pallas as pl
from jax.experimental.pallas import tpu as pltpu
from jax.sharding import Mesh, PartitionSpec as P

F32 = jnp.float32
BF16 = jnp.bfloat16
META = 16
PAIR = 2


def compute_kernel(where_ref, g_ref, h_ref, o_ref, w_ref, s_ref, acc):
    step = pl.program_id(0)
    expert = where_ref[0]
    part = where_ref[1]
    odd = lax.rem(part, 2)
    cols = g_ref.shape[1] - META
    units, cap = h_ref.shape[1:]
    groups, rows, _ = w_ref.shape
    live = units // groups
    width = o_ref.shape[1]
    pad = 8
    meta_row = lax.broadcasted_iota(jnp.int32, (META, cap), 0)
    slot_row = lax.broadcasted_iota(jnp.int32, (cap, cap), 0)
    lhs, rhs = [], []
    for u in range(PAIR):
        meta = g_ref[u, cols:, :].astype(F32)
        slot = jnp.sum(jnp.where(meta_row == expert, meta, 0.0), axis=0, keepdims=True)
        weight = jnp.sum(jnp.where(meta_row == expert + 4, meta, 0.0), axis=0, keepdims=True)
        place = (slot_row == slot.astype(jnp.int32)).astype(BF16)
        hidden = jnp.dot(h_ref[u], place, preferred_element_type=F32)
        out = jnp.dot(o_ref[u], place, preferred_element_type=F32)
        gap = jnp.zeros((pad, cap), F32)
        shifted = jnp.where(
            odd == 1, jnp.concatenate([gap, out], axis=0), jnp.concatenate([out, gap], axis=0)
        )
        start = pl.multiple_of(part * width - pad * odd, 16)
        window = g_ref[u, pl.ds(start, width + pad), :].astype(F32)
        s_ref[0, u : u + 1, :] = jnp.sum(shifted * window, axis=0, keepdims=True)
        blank = jnp.zeros((rows - live, cap), F32)
        spread = []
        for q in range(groups):
            spread += [hidden[q * live : (q + 1) * live], blank]
        lhs.append(jnp.concatenate(spread, axis=0).astype(BF16))
        rhs.append((g_ref[u, :cols, :].astype(F32) * weight).astype(BF16))
    term = lax.dot_general(
        jnp.concatenate(lhs, axis=1),
        jnp.concatenate(rhs, axis=1),
        (((1,), (1,)), ((), ())),
        preferred_element_type=F32,
    )

    @pl.when(step == 0)
    def _():
        acc[...] = term

    @pl.when(step > 0)
    def _():
        acc[...] += term

    @pl.when(step == pl.num_programs(0) - 1)
    def _():
        for q in range(groups):
            w_ref[q] = acc[q * rows : (q + 1) * rows, :].astype(BF16)


def compute(where, g, h, o, groups):
    sources, wide, cap = g.shape
    units = h.shape[1]
    cols = wide - META
    rows = -(-(units // groups) // 16) * 16
    return pl.pallas_call(
        compute_kernel,
        grid_spec=pltpu.PrefetchScalarGridSpec(
            num_scalar_prefetch=1,
            grid=(sources // PAIR,),
            in_specs=[
                pl.BlockSpec((PAIR, wide, cap), lambda i, w: (i, 0, 0)),
                pl.BlockSpec((PAIR, units, cap), lambda i, w: (i, 0, 0)),
                pl.BlockSpec((PAIR, o.shape[1], cap), lambda i, w: (i, 0, 0)),
            ],
            out_specs=[
                pl.BlockSpec((groups, rows, cols), lambda i, w: (0, 0, 0)),
                pl.BlockSpec((1, PAIR, cap), lambda i, w: (i, 0, 0)),
            ],
            scratch_shapes=[pltpu.VMEM((groups * rows, cols), F32)],
        ),
        out_shape=[
            jax.ShapeDtypeStruct((groups, rows, cols), BF16),
            jax.ShapeDtypeStruct((sources // PAIR, PAIR, cap), F32),
        ],
        compiler_params=pltpu.CompilerParams(vmem_limit_bytes=40 * 1024 * 1024),
    )(where, g, h, o)


def local(out_grad, routes, slots, combine_weight, saved_hidden, saved_out):
    nx, nz = lax.axis_size("x"), lax.axis_size("z")
    blocks = lax.axis_size("y") * lax.axis_size("c")
    cap, units = saved_hidden.shape[3:]
    cols = out_grad.shape[1]
    split = cols // saved_out.shape[4]
    experts = blocks // split
    topk = routes.shape[1]
    me = lax.axis_index("y") * lax.axis_size("c") + lax.axis_index("c")
    where = jnp.stack([me // split, me % split]).astype(jnp.int32)

    names = routes.T[None] == jnp.arange(experts, dtype=jnp.int32)[:, None, None]
    slot_of = jnp.sum(jnp.where(names, slots.T[None].astype(F32), 0.0), axis=1)
    weight_of = jnp.sum(jnp.where(names, combine_weight.T[None].astype(F32), 0.0), axis=1)
    meta = jnp.concatenate([slot_of, weight_of, jnp.zeros((META - 2 * experts, slot_of.shape[1]), F32)])
    sent = jnp.concatenate([out_grad.T, meta.astype(BF16)], axis=0)
    gathered = lax.all_gather(sent, ("y", "c"), axis=0)

    h = saved_hidden[0, 0].transpose(0, 2, 1)
    o = saved_out[0, 0].transpose(0, 2, 1)
    term, scores = compute(where, gathered, h, o, nx)

    by_x = lax.all_to_all(term, "x", split_axis=0, concat_axis=0, tiled=True)
    returned = lax.all_to_all(
        scores.reshape(blocks, 1, cap), ("y", "c"), split_axis=0, concat_axis=0, tiled=True
    )
    live = units // nx
    quarter = jnp.sum(by_x.astype(F32), axis=0)[:live].astype(BF16)
    share = live * cols // nz
    block = -(-share // 1024) * 1024
    flat = jnp.pad(quarter.reshape(nz, share), ((0, 0), (0, block - share)))
    by_z = lax.all_to_all(
        flat.reshape(nz, block // 128, 128), "z", split_axis=0, concat_axis=0, tiled=True
    )
    summed = jnp.sum(by_z.astype(F32), axis=0).astype(BF16)
    weight_grad = summed.reshape(1, block)[:, :share]

    combined = jnp.sum(returned.reshape(experts, split, cap), axis=1)
    router_grad = jnp.sum(jnp.where(names, combined[:, None, :], 0.0), axis=0).T
    return (weight_grad, router_grad)


def solution(mesh):
    nx = {64: 4, 4: 2}[mesh.shape["dp"]]
    grid = Mesh(
        mesh.devices.reshape(nx, mesh.shape["dp"] // nx, mesh.shape["expert"] // 2, 2),
        ("x", "z", "y", "c"),
    )
    rows = P(("x", "z", "y", "c"), None)
    saved = P(("x", "z"), ("y", "c"), None, None, None)
    return jax.shard_map(
        local,
        mesh=grid,
        in_specs=(rows, rows, rows, rows, saved, saved),
        out_specs=(P(("y", "c"), ("x", "z")), rows),
        check_vma=False,
    )
```

```python
import jax
import jax.numpy as jnp
from jax import lax
from jax.experimental import pallas as pl
from jax.experimental.pallas import tpu as pltpu
from jax.sharding import Mesh, PartitionSpec as P

F32 = jnp.float32
BF16 = jnp.bfloat16
STEP = 4
SHIFT = 8
SPREAD = 16
VMEM = 56 * 1024 * 1024


def place_kernel(part_ref, meta_ref, h_ref, o_ref, hp_ref, op_ref):
    odd = lax.rem(part_ref[0], 2)
    cap = h_ref.shape[2]
    live, rows = h_ref.shape[1] // NX[0], hp_ref.shape[0] // NX[0]
    slot_row = lax.broadcasted_iota(jnp.int32, (cap, cap), 0)
    gap = jnp.zeros((SHIFT, cap), F32)
    blank = jnp.zeros((rows - live, cap), F32)
    for u in range(STEP):
        slot = meta_ref[u, 0:1, :].astype(jnp.int32)
        place = (slot_row == slot).astype(BF16)
        hidden = jnp.dot(h_ref[u], place, preferred_element_type=F32)
        out = jnp.dot(o_ref[u], place, preferred_element_type=F32)
        op_ref[u] = jnp.where(
            odd == 1, jnp.concatenate([gap, out], axis=0), jnp.concatenate([out, gap], axis=0)
        ).astype(BF16)
        spread = []
        for q in range(NX[0]):
            spread += [hidden[q * live : (q + 1) * live], blank]
        hp_ref[:, u * cap : (u + 1) * cap] = jnp.concatenate(spread, axis=0).astype(BF16)


def term_kernel(part_ref, meta_ref, g_ref, hp_ref, op_ref, w_ref, s_ref, acc):
    step = pl.program_id(0)
    part = part_ref[0]
    width = op_ref.shape[1]
    start = pl.multiple_of(part * (width - SHIFT) - SHIFT * lax.rem(part, 2), 16)
    groups, rows, _ = w_ref.shape
    rhs = []
    for u in range(STEP):
        weight = meta_ref[u, 1:2, :]
        window = g_ref[u, pl.ds(start, width), :].astype(F32)
        score = jnp.sum(op_ref[u].astype(F32) * window, axis=0, keepdims=True)
        s_ref[u] = jnp.broadcast_to(score, s_ref.shape[1:])
        rhs.append((g_ref[u].astype(F32) * weight).astype(BF16))
    term = lax.dot_general(
        hp_ref[...],
        jnp.concatenate(rhs, axis=1),
        (((1,), (1,)), ((), ())),
        preferred_element_type=F32,
    )

    @pl.when(step == 0)
    def _():
        acc[...] = term

    @pl.when(step > 0)
    def _():
        acc[...] += term

    @pl.when(step == pl.num_programs(0) - 1)
    def _():
        for q in range(groups):
            w_ref[q] = acc[q * rows : (q + 1) * rows, :].astype(BF16)


NX = [4]


def place(part, meta, h, o, rows):
    sources, units, cap = h.shape
    width = o.shape[1] + SHIFT
    return pl.pallas_call(
        place_kernel,
        grid_spec=pltpu.PrefetchScalarGridSpec(
            num_scalar_prefetch=1,
            grid=(sources // STEP,),
            in_specs=[
                pl.BlockSpec((STEP, 2, cap), lambda i, p: (i, 0, 0)),
                pl.BlockSpec((STEP, units, cap), lambda i, p: (i, 0, 0)),
                pl.BlockSpec((STEP, o.shape[1], cap), lambda i, p: (i, 0, 0)),
            ],
            out_specs=[
                pl.BlockSpec((NX[0] * rows, STEP * cap), lambda i, p: (0, i)),
                pl.BlockSpec((STEP, width, cap), lambda i, p: (i, 0, 0)),
            ],
        ),
        out_shape=[
            jax.ShapeDtypeStruct((NX[0] * rows, sources * cap), BF16),
            jax.ShapeDtypeStruct((sources, width, cap), BF16),
        ],
        compiler_params=pltpu.CompilerParams(vmem_limit_bytes=VMEM),
        cost_estimate=pl.CostEstimate(
            flops=4 * sources * units * cap * cap, bytes_accessed=8 * sources * units * cap, transcendentals=0
        ),
    )(part, meta, h, o)


def weight_term(part, meta, g, hp, op, rows):
    sources, cols, cap = g.shape
    width = op.shape[1]
    return pl.pallas_call(
        term_kernel,
        grid_spec=pltpu.PrefetchScalarGridSpec(
            num_scalar_prefetch=1,
            grid=(sources // STEP,),
            in_specs=[
                pl.BlockSpec((STEP, 2, cap), lambda i, p: (i, 0, 0)),
                pl.BlockSpec((STEP, cols, cap), lambda i, p: (i, 0, 0)),
                pl.BlockSpec((NX[0] * rows, STEP * cap), lambda i, p: (0, i)),
                pl.BlockSpec((STEP, width, cap), lambda i, p: (i, 0, 0)),
            ],
            out_specs=[
                pl.BlockSpec((NX[0], rows, cols), lambda i, p: (0, 0, 0)),
                pl.BlockSpec((STEP, SPREAD, cap), lambda i, p: (i, 0, 0)),
            ],
            scratch_shapes=[pltpu.VMEM((NX[0] * rows, cols), F32)],
        ),
        out_shape=[
            jax.ShapeDtypeStruct((NX[0], rows, cols), BF16),
            jax.ShapeDtypeStruct((sources, SPREAD, cap), F32),
        ],
        compiler_params=pltpu.CompilerParams(vmem_limit_bytes=VMEM),
        cost_estimate=pl.CostEstimate(
            flops=2 * sources * cap * NX[0] * rows * cols, bytes_accessed=2 * sources * cols * cap, transcendentals=0
        ),
    )(part, meta, g, hp, op)


def local(out_grad, routes, slots, combine_weight, saved_hidden, saved_out):
    nx, nz = lax.axis_size("x"), lax.axis_size("z")
    NX[0] = nx
    blocks = lax.axis_size("y") * lax.axis_size("c")
    cap, units = saved_hidden.shape[3:]
    cols = out_grad.shape[1]
    split = cols // saved_out.shape[4]
    experts = blocks // split
    me = lax.axis_index("y") * lax.axis_size("c") + lax.axis_index("c")
    part = (me % split).reshape(1).astype(jnp.int32)
    live = units // nx
    rows = -(-live // 16) * 16

    gathered = lax.all_gather(out_grad.T, ("y", "c"), axis=0)

    names = routes.T[None] == jnp.arange(experts, dtype=jnp.int32)[:, None, None]
    slot_of = jnp.sum(jnp.where(names, slots.T[None].astype(F32), 0.0), axis=1)
    weight_of = jnp.sum(jnp.where(names, combine_weight.T[None].astype(F32), 0.0), axis=1)
    sent = jnp.repeat(jnp.stack([slot_of, weight_of], axis=1), split, axis=0)
    meta = lax.all_to_all(sent, ("y", "c"), split_axis=0, concat_axis=0, tiled=True)

    h = saved_hidden[0, 0].transpose(0, 2, 1)
    o = saved_out[0, 0].transpose(0, 2, 1)
    hp, op = place(part, meta, h, o, rows)
    term, scores = weight_term(part, meta, gathered, hp, op, rows)

    everyones = lax.all_gather(scores, ("y", "c"), axis=0)
    by_x = lax.all_to_all(term, "x", split_axis=0, concat_axis=0, tiled=True)
    quarter = jnp.sum(by_x.astype(F32), axis=0)[:live].astype(BF16)
    share = live * cols // nz
    block = -(-share // 1024) * 1024
    flat = jnp.pad(quarter.reshape(nz, share), ((0, 0), (0, block - share)))
    by_z = lax.all_to_all(
        flat.reshape(nz, block // 128, 128), "z", split_axis=0, concat_axis=0, tiled=True
    )
    summed = jnp.sum(by_z.astype(F32), axis=0).astype(BF16)
    weight_grad = summed.reshape(1, block)[:, :share]

    returned = lax.dynamic_slice_in_dim(everyones, me, 1, axis=1)[:, 0, 0]
    combined = jnp.sum(returned.reshape(experts, split, cap), axis=1)
    router_grad = jnp.sum(jnp.where(names, combined[:, None, :], 0.0), axis=0).T
    return (weight_grad, router_grad)


def solution(mesh):
    nx = {64: 4, 4: 2}[mesh.shape["dp"]]
    grid = Mesh(
        mesh.devices.reshape(nx, mesh.shape["dp"] // nx, mesh.shape["expert"] // 2, 2),
        ("x", "z", "y", "c"),
    )
    rows = P(("x", "z", "y", "c"), None)
    saved = P(("x", "z"), ("y", "c"), None, None, None)
    return jax.shard_map(
        local,
        mesh=grid,
        in_specs=(rows, rows, rows, rows, saved, saved),
        out_specs=(P(("y", "c"), ("x", "z")), rows),
        check_vma=False,
    )
```

```python
import functools

import jax
import jax.numpy as jnp
from jax import lax
from jax.experimental import pallas as pl
from jax.experimental.pallas import tpu as pltpu
from jax.sharding import Mesh, PartitionSpec as P

F32 = jnp.float32
BF16 = jnp.bfloat16
STEP = 4
SHIFT = 8
SPREAD = 16
FOLD = 4
LANE = 128
TILE = 256
VMEM = 56 * 1024 * 1024


def place_kernel(part_ref, meta_ref, h_ref, o_ref, hp_ref, op_ref, tall):
    odd = lax.rem(part_ref[0], 2)
    units, cap = h_ref.shape[1:]
    rows = hp_ref.shape[0] // FOLD
    slot_row = lax.broadcasted_iota(jnp.int32, (cap, cap), 0)
    gap = jnp.zeros((SHIFT, cap), F32)
    blank = jnp.zeros((rows - units // FOLD, cap), F32)
    for u in range(STEP):
        slot = meta_ref[u, 0:1, :].astype(jnp.int32)
        place = (slot_row == slot).astype(BF16)
        tall[...] = jnp.dot(h_ref[u], place, preferred_element_type=F32)
        out = jnp.dot(o_ref[u], place, preferred_element_type=F32)
        op_ref[u] = jnp.where(
            odd == 1, jnp.concatenate([gap, out], axis=0), jnp.concatenate([out, gap], axis=0)
        ).astype(BF16)
        for m in range(FOLD):
            picked = tall[pl.ds(m, units // FOLD, stride=FOLD), :]
            hp_ref[m * rows : (m + 1) * rows, u * cap : (u + 1) * cap] = jnp.concatenate(
                [picked, blank], axis=0
            ).astype(BF16)


def term_kernel(shape, part_ref, meta_ref, g_ref, hp_ref, op_ref, w_ref, s_ref, acc, rhs, flat):
    units, nx, nh, nl = shape
    step = pl.program_id(0)
    part = part_ref[0]
    width = op_ref.shape[1]
    cols, cap = g_ref.shape[1:]
    wide = rhs.shape[0]
    start = pl.multiple_of(part * (width - SHIFT) - SHIFT * lax.rem(part, 2), 16)

    @pl.when(step == 0)
    def _():
        rhs[cols:, :] = jnp.zeros((wide - cols, STEP * cap), BF16)

    for u in range(STEP):
        weight = meta_ref[u, 1:2, :]
        window = g_ref[u, pl.ds(start, width), :].astype(F32)
        score = jnp.sum(op_ref[u].astype(F32) * window, axis=0, keepdims=True)
        s_ref[u] = jnp.broadcast_to(score, s_ref.shape[1:])
        rhs[:cols, u * cap : (u + 1) * cap] = (g_ref[u].astype(F32) * weight).astype(BF16)

    def add(first):
        for n in range(0, wide, TILE):
            term = lax.dot_general(
                hp_ref[...],
                rhs[n : n + TILE, :],
                (((1,), (1,)), ((), ())),
                preferred_element_type=F32,
            )
            acc[:, n : n + TILE] = term if first else acc[:, n : n + TILE] + term

    pl.when(step == 0)(lambda: add(True))
    pl.when(step > 0)(lambda: add(False))

    @pl.when(step == pl.num_programs(0) - 1)
    def _():
        live, rows = units // FOLD, acc.shape[0] // FOLD
        span = FOLD * cols // LANE
        whole = units * cols // LANE
        flat[whole:, :] = jnp.zeros((flat.shape[0] - whole, LANE), F32)
        tail = None
        for m in range(FOLD):
            lead, offset = divmod(m * cols, LANE)
            lines = acc[m * rows : (m + 1) * rows, :]
            lines = pltpu.roll(lines, offset, 1) if offset else lines
            for t in range(wide // LANE):
                piece = lines[:live, t * LANE : (t + 1) * LANE]
                if t == 0 and offset:
                    piece = piece + tail
                tail = piece
                end = (lead + t + 1) * LANE
                if end <= (m + 1) * cols:
                    flat[pl.ds(lead + t, live, stride=span), :] = piece
                elif end - LANE < (m + 1) * cols:
                    break
        size = w_ref.shape[1] // nh
        share = units * cols // (nx * nh * nl)
        lane = lax.broadcasted_iota(jnp.int32, (size, LANE), 1)
        for q in range(nx * nh * nl):
            x, z = divmod(q, nh * nl)
            base, offset = divmod(q * share, LANE)
            own = flat[base : base + size, :]
            if offset:
                after = flat[base + 1 : base + 1 + size, :]
                own = pltpu.roll(jnp.where(lane < offset, after, own), LANE - offset, 1)
            h, l = divmod(z, nl)
            w_ref[x * nl + l, h * size : (h + 1) * size, :] = own.astype(BF16)


def place(part, meta, h, o, rows):
    sources, units, cap = h.shape
    width = o.shape[1] + SHIFT
    return pl.pallas_call(
        place_kernel,
        grid_spec=pltpu.PrefetchScalarGridSpec(
            num_scalar_prefetch=1,
            grid=(sources // STEP,),
            in_specs=[
                pl.BlockSpec((STEP, 2, cap), lambda i, p: (i, 0, 0)),
                pl.BlockSpec((STEP, units, cap), lambda i, p: (i, 0, 0)),
                pl.BlockSpec((STEP, o.shape[1], cap), lambda i, p: (i, 0, 0)),
            ],
            out_specs=[
                pl.BlockSpec((FOLD * rows, STEP * cap), lambda i, p: (0, i)),
                pl.BlockSpec((STEP, width, cap), lambda i, p: (i, 0, 0)),
            ],
            scratch_shapes=[pltpu.VMEM((units, cap), F32)],
        ),
        out_shape=[
            jax.ShapeDtypeStruct((FOLD * rows, sources * cap), BF16),
            jax.ShapeDtypeStruct((sources, width, cap), BF16),
        ],
        compiler_params=pltpu.CompilerParams(vmem_limit_bytes=VMEM),
        cost_estimate=pl.CostEstimate(
            flops=4 * sources * units * cap * cap, bytes_accessed=8 * sources * units * cap, transcendentals=0
        ),
    )(part, meta, h, o)


def weight_term(part, meta, g, hp, op, shape):
    units, nx, nh, nl = shape
    sources, cols, cap = g.shape
    width = op.shape[1]
    high = hp.shape[0]
    wide = -(-cols // TILE) * TILE
    share = units * cols // (nx * nh * nl)
    size = -(-share // (16 * LANE)) * 16
    lines = -(-((nx * nh * nl - 1) * share // LANE + size + 1) // 8) * 8
    return pl.pallas_call(
        functools.partial(term_kernel, shape),
        grid_spec=pltpu.PrefetchScalarGridSpec(
            num_scalar_prefetch=1,
            grid=(sources // STEP,),
            in_specs=[
                pl.BlockSpec((STEP, 2, cap), lambda i, p: (i, 0, 0)),
                pl.BlockSpec((STEP, cols, cap), lambda i, p: (i, 0, 0)),
                pl.BlockSpec((high, STEP * cap), lambda i, p: (0, i)),
                pl.BlockSpec((STEP, width, cap), lambda i, p: (i, 0, 0)),
            ],
            out_specs=[
                pl.BlockSpec((nx * nl, nh * size, LANE), lambda i, p: (0, 0, 0)),
                pl.BlockSpec((STEP, SPREAD, cap), lambda i, p: (i, 0, 0)),
            ],
            scratch_shapes=[
                pltpu.VMEM((high, wide), F32),
                pltpu.VMEM((wide, STEP * cap), BF16),
                pltpu.VMEM((lines, LANE), F32),
            ],
        ),
        out_shape=[
            jax.ShapeDtypeStruct((nx * nl, nh * size, LANE), BF16),
            jax.ShapeDtypeStruct((sources, SPREAD, cap), F32),
        ],
        compiler_params=pltpu.CompilerParams(vmem_limit_bytes=VMEM),
        cost_estimate=pl.CostEstimate(
            flops=2 * sources * cap * high * wide, bytes_accessed=2 * sources * cols * cap, transcendentals=0
        ),
    )(part, meta, g, hp, op)


def local(out_grad, routes, slots, combine_weight, saved_hidden, saved_out):
    nx, nh, nl = (lax.axis_size(name) for name in ("x", "zh", "zl"))
    blocks = lax.axis_size("y") * lax.axis_size("c")
    cap, units = saved_hidden.shape[3:]
    cols = out_grad.shape[1]
    split = cols // saved_out.shape[4]
    experts = blocks // split
    me = lax.axis_index("y") * lax.axis_size("c") + lax.axis_index("c")
    part = (me % split).reshape(1).astype(jnp.int32)
    rows = -(-(units // FOLD) // 16) * 16

    gathered = lax.all_gather(out_grad.T, ("y", "c"), axis=0)

    names = routes.T[None] == jnp.arange(experts, dtype=jnp.int32)[:, None, None]
    slot_of = jnp.sum(jnp.where(names, slots.T[None].astype(F32), 0.0), axis=1)
    weight_of = jnp.sum(jnp.where(names, combine_weight.T[None].astype(F32), 0.0), axis=1)
    sent = jnp.repeat(jnp.stack([slot_of, weight_of], axis=1), split, axis=0)
    meta = lax.all_to_all(sent, ("y", "c"), split_axis=0, concat_axis=0, tiled=True)

    h = saved_hidden[0, 0].transpose(0, 2, 1)
    o = saved_out[0, 0].transpose(0, 2, 1)
    hp, op = place(part, meta, h, o, rows)
    term, scores = weight_term(part, meta, gathered, hp, op, (units, nx, nh, nl))

    everyones = lax.all_gather(scores, ("y", "c"), axis=0)
    first = lax.all_to_all(term, ("x", "zl"), split_axis=0, concat_axis=0, tiled=True)
    partial_sum = jnp.sum(first.astype(F32), axis=0).astype(BF16)
    second = lax.all_to_all(
        partial_sum.reshape(nh, -1, LANE), "zh", split_axis=0, concat_axis=0, tiled=True
    )
    summed = jnp.sum(second.astype(F32), axis=0).astype(BF16)
    weight_grad = summed.reshape(1, -1)[:, : units * cols // (nx * nh * nl)]

    returned = lax.dynamic_slice_in_dim(everyones, me, 1, axis=1)[:, 0, 0]
    combined = jnp.sum(returned.reshape(experts, split, cap), axis=1)
    router_grad = jnp.sum(jnp.where(names, combined[:, None, :], 0.0), axis=0).T
    return (weight_grad, router_grad)


def solution(mesh):
    nx = {64: 4, 4: 2}[mesh.shape["dp"]]
    grid = Mesh(
        mesh.devices.reshape(nx, mesh.shape["dp"] // nx // 2, 2, mesh.shape["expert"] // 2, 2),
        ("x", "zh", "zl", "y", "c"),
    )
    rows = P(("x", "zh", "zl", "y", "c"), None)
    saved = P(("x", "zh", "zl"), ("y", "c"), None, None, None)
    return jax.shard_map(
        local,
        mesh=grid,
        in_specs=(rows, rows, rows, rows, saved, saved),
        out_specs=(P(("y", "c"), ("x", "zh", "zl")), rows),
        check_vma=False,
    )
```

```python
import functools

import jax
import jax.numpy as jnp
from jax import lax
from jax.experimental import pallas as pl
from jax.experimental.pallas import tpu as pltpu
from jax.sharding import Mesh, PartitionSpec as P

F32 = jnp.float32
BF16 = jnp.bfloat16
STEP = 4
SHIFT = 8
SPREAD = 16
FOLD = 4
LANE = 128
TILE = 256
VMEM = 56 * 1024 * 1024


def place_kernel(part_ref, meta_ref, h_ref, o_ref, hp_ref, op_ref, tall):
    odd = lax.rem(part_ref[0], 2)
    units, cap = h_ref.shape[1:]
    rows = hp_ref.shape[1] // FOLD
    slot_row = lax.broadcasted_iota(jnp.int32, (cap, cap), 0)
    gap = jnp.zeros((SHIFT, cap), F32)
    blank = jnp.zeros((rows - units // FOLD, cap), F32)
    for u in range(STEP):
        slot = meta_ref[u, 0:1, :].astype(jnp.int32)
        place = (slot_row == slot).astype(BF16)
        tall[...] = jnp.dot(h_ref[u], place, preferred_element_type=F32)
        out = jnp.dot(o_ref[u], place, preferred_element_type=F32)
        op_ref[u] = jnp.where(
            odd == 1, jnp.concatenate([gap, out], axis=0), jnp.concatenate([out, gap], axis=0)
        ).astype(BF16)
        for m in range(FOLD):
            picked = tall[pl.ds(m, units // FOLD, stride=FOLD), :]
            hp_ref[0, m * rows : (m + 1) * rows, u * cap : (u + 1) * cap] = jnp.concatenate(
                [picked, blank], axis=0
            ).astype(BF16)


def score_kernel(part_ref, g_ref, op_ref, s_ref, window, out, arrived):
    sources, width, _ = out.shape
    part = part_ref[0]
    start = pl.multiple_of(part * (width - SHIFT) - SHIFT * lax.rem(part, 2), 16)
    copies = []
    for i in range(sources // STEP):
        some = slice(i * STEP, (i + 1) * STEP)
        copies.append(
            (
                pltpu.make_async_copy(
                    g_ref.at[some, pl.ds(start, width), :], window.at[some], arrived.at[i, 0]
                ),
                pltpu.make_async_copy(op_ref.at[some], out.at[some], arrived.at[i, 1]),
            )
        )
    for pair in copies:
        for copy in pair:
            copy.start()
    for i, pair in enumerate(copies):
        for copy in pair:
            copy.wait()
        for u in range(i * STEP, (i + 1) * STEP):
            score = jnp.sum(out[u].astype(F32) * window[u].astype(F32), axis=0, keepdims=True)
            s_ref[u] = jnp.broadcast_to(score, s_ref.shape[1:])


def term_kernel(shape, meta_ref, g_ref, hp_ref, w_ref, acc, rhs, flat, grads, hidden, arrived):
    units, nx, nh, nl = shape
    sources, cols, cap = grads.shape
    wide = rhs.shape[0]
    copies = []
    for i in range(sources // STEP):
        copies.append([pltpu.make_async_copy(hp_ref.at[i], hidden.at[i], arrived.at[i, STEP])])
        for u in range(STEP):
            j = i * STEP + u
            copies[-1].append(pltpu.make_async_copy(g_ref.at[j], grads.at[j], arrived.at[i, u]))
    for group in copies:
        for copy in group:
            copy.start()
    rhs[cols:, :] = jnp.zeros((wide - cols, STEP * cap), BF16)
    for i, group in enumerate(copies):
        for copy in group:
            copy.wait()
        for u in range(STEP):
            j = i * STEP + u
            weight = meta_ref[j, 1:2, :]
            rhs[:cols, u * cap : (u + 1) * cap] = (grads[j].astype(F32) * weight).astype(BF16)
        for n in range(0, wide, TILE):
            term = lax.dot_general(
                hidden[i],
                rhs[n : n + TILE, :],
                (((1,), (1,)), ((), ())),
                preferred_element_type=F32,
            )
            acc[:, n : n + TILE] = term if i == 0 else acc[:, n : n + TILE] + term

    live, rows = units // FOLD, acc.shape[0] // FOLD
    span = FOLD * cols // LANE
    whole = units * cols // LANE
    flat[whole:, :] = jnp.zeros((flat.shape[0] - whole, LANE), F32)
    tail = None
    for m in range(FOLD):
        lead, offset = divmod(m * cols, LANE)
        lines = acc[m * rows : (m + 1) * rows, :]
        lines = pltpu.roll(lines, offset, 1) if offset else lines
        for t in range(wide // LANE):
            piece = lines[:live, t * LANE : (t + 1) * LANE]
            if t == 0 and offset:
                piece = piece + tail
            tail = piece
            end = (lead + t + 1) * LANE
            if end <= (m + 1) * cols:
                flat[pl.ds(lead + t, live, stride=span), :] = piece
            elif end - LANE < (m + 1) * cols:
                break
    size = w_ref.shape[1] // nh
    share = units * cols // (nx * nh * nl)
    lane = lax.broadcasted_iota(jnp.int32, (size, LANE), 1)
    for q in range(nx * nh * nl):
        x, z = divmod(q, nh * nl)
        base, offset = divmod(q * share, LANE)
        own = flat[base : base + size, :]
        if offset:
            after = flat[base + 1 : base + 1 + size, :]
            own = pltpu.roll(jnp.where(lane < offset, after, own), LANE - offset, 1)
        h, l = divmod(z, nl)
        w_ref[x * nl + l, h * size : (h + 1) * size, :] = own.astype(BF16)


def place(part, meta, h, o, rows):
    sources, units, cap = h.shape
    width = o.shape[1] + SHIFT
    return pl.pallas_call(
        place_kernel,
        grid_spec=pltpu.PrefetchScalarGridSpec(
            num_scalar_prefetch=1,
            grid=(sources // STEP,),
            in_specs=[
                pl.BlockSpec((STEP, 2, cap), lambda i, p: (i, 0, 0)),
                pl.BlockSpec((STEP, units, cap), lambda i, p: (i, 0, 0)),
                pl.BlockSpec((STEP, o.shape[1], cap), lambda i, p: (i, 0, 0)),
            ],
            out_specs=[
                pl.BlockSpec((1, FOLD * rows, STEP * cap), lambda i, p: (i, 0, 0)),
                pl.BlockSpec((STEP, width, cap), lambda i, p: (i, 0, 0)),
            ],
            scratch_shapes=[pltpu.VMEM((units, cap), F32)],
        ),
        out_shape=[
            jax.ShapeDtypeStruct((sources // STEP, FOLD * rows, STEP * cap), BF16),
            jax.ShapeDtypeStruct((sources, width, cap), BF16),
        ],
        compiler_params=pltpu.CompilerParams(vmem_limit_bytes=VMEM),
        cost_estimate=pl.CostEstimate(
            flops=4 * sources * units * cap * cap, bytes_accessed=8 * sources * units * cap, transcendentals=0
        ),
    )(part, meta, h, o)


def scores_of(part, g, op):
    sources, width, cap = op.shape
    return pl.pallas_call(
        score_kernel,
        in_specs=[
            pl.BlockSpec(memory_space=pltpu.SMEM),
            pl.BlockSpec(memory_space=pl.ANY),
            pl.BlockSpec(memory_space=pl.ANY),
        ],
        out_shape=jax.ShapeDtypeStruct((sources, SPREAD, cap), F32),
        scratch_shapes=[
            pltpu.VMEM((sources, width, cap), BF16),
            pltpu.VMEM((sources, width, cap), BF16),
            pltpu.SemaphoreType.DMA((sources // STEP, 2)),
        ],
        compiler_params=pltpu.CompilerParams(vmem_limit_bytes=VMEM),
        cost_estimate=pl.CostEstimate(
            flops=2 * sources * width * cap, bytes_accessed=4 * sources * width * cap, transcendentals=0
        ),
    )(part, g, op)


def weight_term(meta, g, hp, shape):
    units, nx, nh, nl = shape
    sources, cols, cap = g.shape
    high = hp.shape[1]
    wide = -(-cols // TILE) * TILE
    share = units * cols // (nx * nh * nl)
    size = -(-share // (16 * LANE)) * 16
    lines = -(-((nx * nh * nl - 1) * share // LANE + size + 1) // 8) * 8
    return pl.pallas_call(
        functools.partial(term_kernel, shape),
        in_specs=[
            pl.BlockSpec(memory_space=pltpu.VMEM),
            pl.BlockSpec(memory_space=pl.ANY),
            pl.BlockSpec(memory_space=pl.ANY),
        ],
        out_specs=pl.BlockSpec(memory_space=pltpu.VMEM),
        out_shape=jax.ShapeDtypeStruct((nx * nl, nh * size, LANE), BF16),
        scratch_shapes=[
            pltpu.VMEM((high, wide), F32),
            pltpu.VMEM((wide, STEP * cap), BF16),
            pltpu.VMEM((lines, LANE), F32),
            pltpu.VMEM((sources, cols, cap), BF16),
            pltpu.VMEM(hp.shape, BF16),
            pltpu.SemaphoreType.DMA((sources // STEP, STEP + 1)),
        ],
        compiler_params=pltpu.CompilerParams(vmem_limit_bytes=VMEM),
        cost_estimate=pl.CostEstimate(
            flops=2 * sources * cap * high * wide, bytes_accessed=2 * sources * cols * cap, transcendentals=0
        ),
    )(meta, g, hp)


def local(out_grad, routes, slots, combine_weight, saved_hidden, saved_out):
    nx, nh, nl = (lax.axis_size(name) for name in ("x", "zh", "zl"))
    blocks = lax.axis_size("y") * lax.axis_size("c")
    cap, units = saved_hidden.shape[3:]
    cols = out_grad.shape[1]
    split = cols // saved_out.shape[4]
    experts = blocks // split
    me = lax.axis_index("y") * lax.axis_size("c") + lax.axis_index("c")
    part = (me % split).reshape(1).astype(jnp.int32)
    rows = -(-(units // FOLD) // 16) * 16

    gathered = lax.all_gather(out_grad.T, ("y", "c"), axis=0)

    names = routes.T[None] == jnp.arange(experts, dtype=jnp.int32)[:, None, None]
    slot_of = jnp.sum(jnp.where(names, slots.T[None].astype(F32), 0.0), axis=1)
    weight_of = jnp.sum(jnp.where(names, combine_weight.T[None].astype(F32), 0.0), axis=1)
    sent = jnp.repeat(jnp.stack([slot_of, weight_of], axis=1), split, axis=0)
    meta = lax.all_to_all(sent, ("y", "c"), split_axis=0, concat_axis=0, tiled=True)

    h = saved_hidden[0, 0].transpose(0, 2, 1)
    o = saved_out[0, 0].transpose(0, 2, 1)
    hp, op = place(part, meta, h, o, rows)
    scores = scores_of(part, gathered, op)
    gathered, scores = lax.optimization_barrier((gathered, scores))
    everyones = lax.all_gather(scores, ("y", "c"), axis=0)
    term = weight_term(meta, gathered, hp, (units, nx, nh, nl))
    first = lax.all_to_all(term, ("x", "zl"), split_axis=0, concat_axis=0, tiled=True)
    partial_sum = jnp.sum(first.astype(F32), axis=0).astype(BF16)
    second = lax.all_to_all(
        partial_sum.reshape(nh, -1, LANE), "zh", split_axis=0, concat_axis=0, tiled=True
    )
    summed = jnp.sum(second.astype(F32), axis=0).astype(BF16)
    weight_grad = summed.reshape(1, -1)[:, : units * cols // (nx * nh * nl)]

    returned = lax.dynamic_slice_in_dim(everyones, me, 1, axis=1)[:, 0, 0]
    combined = jnp.sum(returned.reshape(experts, split, cap), axis=1)
    router_grad = jnp.sum(jnp.where(names, combined[:, None, :], 0.0), axis=0).T
    return (weight_grad, router_grad)


def solution(mesh):
    nx = {64: 4, 4: 2}[mesh.shape["dp"]]
    grid = Mesh(
        mesh.devices.reshape(nx, mesh.shape["dp"] // nx // 2, 2, mesh.shape["expert"] // 2, 2),
        ("x", "zh", "zl", "y", "c"),
    )
    rows = P(("x", "zh", "zl", "y", "c"), None)
    saved = P(("x", "zh", "zl"), ("y", "c"), None, None, None)
    return jax.shard_map(
        local,
        mesh=grid,
        in_specs=(rows, rows, rows, rows, saved, saved),
        out_specs=(P(("y", "c"), ("x", "zh", "zl")), rows),
        check_vma=False,
    )
```

```python
import functools

import jax
import jax.numpy as jnp
from jax import lax
from jax.experimental import pallas as pl
from jax.experimental.pallas import tpu as pltpu
from jax.sharding import Mesh, PartitionSpec as P

F32 = jnp.float32
BF16 = jnp.bfloat16
STEP = 4
SHIFT = 8
SPREAD = 16
FOLD = 4
LANE = 128
TILE = 256
VMEM = 56 * 1024 * 1024


def place_kernel(part_ref, meta_ref, h_ref, o_ref, hp_ref, op_ref, tall):
    odd = lax.rem(part_ref[0], 2)
    units, cap = h_ref.shape[1:]
    rows = hp_ref.shape[1] // FOLD
    slot_row = lax.broadcasted_iota(jnp.int32, (cap, cap), 0)
    gap = jnp.zeros((SHIFT, cap), F32)
    blank = jnp.zeros((rows - units // FOLD, cap), F32)
    for u in range(STEP):
        slot = meta_ref[u, 0:1, :].astype(jnp.int32)
        place = (slot_row == slot).astype(BF16)
        tall[...] = jnp.dot(h_ref[u], place, preferred_element_type=F32)
        out = jnp.dot(o_ref[u], place, preferred_element_type=F32)
        op_ref[u] = jnp.where(
            odd == 1, jnp.concatenate([gap, out], axis=0), jnp.concatenate([out, gap], axis=0)
        ).astype(BF16)
        for m in range(FOLD):
            picked = tall[pl.ds(m, units // FOLD, stride=FOLD), :]
            hp_ref[0, m * rows : (m + 1) * rows, u * cap : (u + 1) * cap] = jnp.concatenate(
                [picked, blank], axis=0
            ).astype(BF16)


def term_kernel(
    shape, part_ref, meta_ref, g_ref, hp_ref, op_ref, w_ref, s_ref,
    acc, rhs, flat, grads, hidden, out, owned, arrived, left,
):
    units, nx, nh, nl = shape
    part = part_ref[0]
    width = out.shape[1]
    start = pl.multiple_of(part * (width - SHIFT) - SHIFT * lax.rem(part, 2), 16)
    sources, cols, cap = grads.shape
    wide = rhs.shape[0]
    copies = []
    for i in range(sources // STEP):
        copies.append([pltpu.make_async_copy(hp_ref.at[i], hidden.at[i], arrived.at[i, STEP])])
        for u in range(STEP):
            j = i * STEP + u
            copies[-1].append(pltpu.make_async_copy(g_ref.at[j], grads.at[j], arrived.at[i, u]))
        some = slice(i * STEP, (i + 1) * STEP)
        copies[-1].append(
            pltpu.make_async_copy(op_ref.at[some], out.at[some], arrived.at[i, STEP + 1])
        )
    for group in copies:
        for copy in group:
            copy.start()
    rhs[cols:, :] = jnp.zeros((wide - cols, STEP * cap), BF16)
    for i, group in enumerate(copies):
        for copy in group:
            copy.wait()
        for u in range(STEP):
            j = i * STEP + u
            weight = meta_ref[j, 1:2, :]
            window = grads[j, pl.ds(start, width), :].astype(F32)
            score = jnp.sum(out[j].astype(F32) * window, axis=0, keepdims=True)
            s_ref[j] = jnp.broadcast_to(score, s_ref.shape[1:])
            rhs[:cols, u * cap : (u + 1) * cap] = (grads[j].astype(F32) * weight).astype(BF16)
        for n in range(0, wide, TILE):
            term = lax.dot_general(
                hidden[i],
                rhs[n : n + TILE, :],
                (((1,), (1,)), ((), ())),
                preferred_element_type=F32,
            )
            acc[:, n : n + TILE] = term if i == 0 else acc[:, n : n + TILE] + term

    live, rows = units // FOLD, acc.shape[0] // FOLD
    span = FOLD * cols // LANE
    whole = units * cols // LANE
    flat[whole:, :] = jnp.zeros((flat.shape[0] - whole, LANE), F32)
    tail = None
    for m in range(FOLD):
        lead, offset = divmod(m * cols, LANE)
        lines = acc[m * rows : (m + 1) * rows, :]
        lines = pltpu.roll(lines, offset, 1) if offset else lines
        for t in range(wide // LANE):
            piece = lines[:live, t * LANE : (t + 1) * LANE]
            if t == 0 and offset:
                piece = piece + tail
            tail = piece
            end = (lead + t + 1) * LANE
            if end <= (m + 1) * cols:
                flat[pl.ds(lead + t, live, stride=span), :] = piece
            elif end - LANE < (m + 1) * cols:
                break
    size = owned.shape[1] // nh
    share = units * cols // (nx * nh * nl)
    lane = lax.broadcasted_iota(jnp.int32, (size, LANE), 1)
    leaving = []
    for dest in range(nx * nl):
        x, l = divmod(dest, nl)
        for h in range(nh):
            base, offset = divmod(((x * nh + h) * nl + l) * share, LANE)
            own = flat[base : base + size, :]
            if offset:
                after = flat[base + 1 : base + 1 + size, :]
                own = pltpu.roll(jnp.where(lane < offset, after, own), LANE - offset, 1)
            owned[dest, h * size : (h + 1) * size, :] = own.astype(BF16)
        leaving.append(pltpu.make_async_copy(owned.at[dest], w_ref.at[dest], left.at[dest]))
        leaving[-1].start()
    for copy in leaving:
        copy.wait()


def place(part, meta, h, o, rows):
    sources, units, cap = h.shape
    width = o.shape[1] + SHIFT
    return pl.pallas_call(
        place_kernel,
        grid_spec=pltpu.PrefetchScalarGridSpec(
            num_scalar_prefetch=1,
            grid=(sources // STEP,),
            in_specs=[
                pl.BlockSpec((STEP, 2, cap), lambda i, p: (i, 0, 0)),
                pl.BlockSpec((STEP, units, cap), lambda i, p: (i, 0, 0)),
                pl.BlockSpec((STEP, o.shape[1], cap), lambda i, p: (i, 0, 0)),
            ],
            out_specs=[
                pl.BlockSpec((1, FOLD * rows, STEP * cap), lambda i, p: (i, 0, 0)),
                pl.BlockSpec((STEP, width, cap), lambda i, p: (i, 0, 0)),
            ],
            scratch_shapes=[pltpu.VMEM((units, cap), F32)],
        ),
        out_shape=[
            jax.ShapeDtypeStruct((sources // STEP, FOLD * rows, STEP * cap), BF16),
            jax.ShapeDtypeStruct((sources, width, cap), BF16),
        ],
        compiler_params=pltpu.CompilerParams(vmem_limit_bytes=VMEM),
        cost_estimate=pl.CostEstimate(
            flops=4 * sources * units * cap * cap, bytes_accessed=8 * sources * units * cap, transcendentals=0
        ),
    )(part, meta, h, o)


def weight_term(part, meta, g, hp, op, shape):
    units, nx, nh, nl = shape
    sources, cols, cap = g.shape
    high = hp.shape[1]
    wide = -(-cols // TILE) * TILE
    share = units * cols // (nx * nh * nl)
    size = -(-share // (16 * LANE)) * 16
    lines = -(-((nx * nh * nl - 1) * share // LANE + size + 1) // 8) * 8
    return pl.pallas_call(
        functools.partial(term_kernel, shape),
        in_specs=[
            pl.BlockSpec(memory_space=pltpu.SMEM),
            pl.BlockSpec(memory_space=pltpu.VMEM),
            pl.BlockSpec(memory_space=pl.ANY),
            pl.BlockSpec(memory_space=pl.ANY),
            pl.BlockSpec(memory_space=pl.ANY),
        ],
        out_specs=[
            pl.BlockSpec(memory_space=pl.ANY),
            pl.BlockSpec(memory_space=pltpu.VMEM),
        ],
        out_shape=[
            jax.ShapeDtypeStruct((nx * nl, nh * size, LANE), BF16),
            jax.ShapeDtypeStruct((sources, SPREAD, cap), F32),
        ],
        scratch_shapes=[
            pltpu.VMEM((high, wide), F32),
            pltpu.VMEM((wide, STEP * cap), BF16),
            pltpu.VMEM((lines, LANE), F32),
            pltpu.VMEM((sources, cols, cap), BF16),
            pltpu.VMEM(hp.shape, BF16),
            pltpu.VMEM(op.shape, BF16),
            pltpu.VMEM((nx * nl, nh * size, LANE), BF16),
            pltpu.SemaphoreType.DMA((sources // STEP, STEP + 2)),
            pltpu.SemaphoreType.DMA((nx * nl,)),
        ],
        compiler_params=pltpu.CompilerParams(vmem_limit_bytes=VMEM),
        cost_estimate=pl.CostEstimate(
            flops=2 * sources * cap * high * wide, bytes_accessed=2 * sources * cols * cap, transcendentals=0
        ),
    )(part, meta, g, hp, op)


def local(out_grad, routes, slots, combine_weight, saved_hidden, saved_out):
    nx, nh, nl = (lax.axis_size(name) for name in ("x", "zh", "zl"))
    blocks = lax.axis_size("y") * lax.axis_size("c")
    cap, units = saved_hidden.shape[3:]
    cols = out_grad.shape[1]
    split = cols // saved_out.shape[4]
    experts = blocks // split
    me = lax.axis_index("y") * lax.axis_size("c") + lax.axis_index("c")
    part = (me % split).reshape(1).astype(jnp.int32)
    rows = -(-(units // FOLD) // 16) * 16

    gathered = lax.all_gather(out_grad.T, ("y", "c"), axis=0)

    names = routes.T[None] == jnp.arange(experts, dtype=jnp.int32)[:, None, None]
    slot_of = jnp.sum(jnp.where(names, slots.T[None].astype(F32), 0.0), axis=1)
    weight_of = jnp.sum(jnp.where(names, combine_weight.T[None].astype(F32), 0.0), axis=1)
    sent = jnp.repeat(jnp.stack([slot_of, weight_of], axis=1), split, axis=0)
    meta = lax.all_to_all(sent, ("y", "c"), split_axis=0, concat_axis=0, tiled=True)

    h = saved_hidden[0, 0].transpose(0, 2, 1)
    o = saved_out[0, 0].transpose(0, 2, 1)
    hp, op = place(part, meta, h, o, rows)
    term, scores = weight_term(part, meta, gathered, hp, op, (units, nx, nh, nl))
    everyones = lax.all_gather(scores, ("y", "c"), axis=0)

    first = lax.all_to_all(term, ("x", "zl"), split_axis=0, concat_axis=0, tiled=True)
    partial_sum = jnp.sum(first.astype(F32), axis=0).astype(BF16)
    second = lax.all_to_all(
        partial_sum.reshape(nh, -1, LANE), "zh", split_axis=0, concat_axis=0, tiled=True
    )
    returned = lax.dynamic_slice_in_dim(everyones, me, 1, axis=1)[:, 0, 0]
    combined = jnp.sum(returned.reshape(experts, split, cap), axis=1)
    router_grad = jnp.sum(jnp.where(names, combined[:, None, :], 0.0), axis=0).T
    second, router_grad = lax.optimization_barrier((second, router_grad))

    summed = jnp.sum(second.astype(F32), axis=0).astype(BF16)
    weight_grad = summed.reshape(1, -1)[:, : units * cols // (nx * nh * nl)]
    return (weight_grad, router_grad)


def solution(mesh):
    nx = {64: 4, 4: 2}[mesh.shape["dp"]]
    grid = Mesh(
        mesh.devices.reshape(nx, mesh.shape["dp"] // nx // 2, 2, mesh.shape["expert"] // 2, 2),
        ("x", "zh", "zl", "y", "c"),
    )
    rows = P(("x", "zh", "zl", "y", "c"), None)
    saved = P(("x", "zh", "zl"), ("y", "c"), None, None, None)
    return jax.shard_map(
        local,
        mesh=grid,
        in_specs=(rows, rows, rows, rows, saved, saved),
        out_specs=(P(("y", "c"), ("x", "zh", "zl")), rows),
        check_vma=False,
    )
```

```python
import functools

import jax
import jax.numpy as jnp
from jax import lax
from jax.experimental import pallas as pl
from jax.experimental.pallas import tpu as pltpu
from jax.sharding import Mesh, PartitionSpec as P

F32 = jnp.float32
BF16 = jnp.bfloat16
STEP = 4
SHIFT = 8
SPREAD = 16
FOLD = 4
LANE = 128
TILE = 256
VMEM = 56 * 1024 * 1024


def place_kernel(part_ref, meta_ref, h_ref, o_ref, hp_ref, op_ref, tall):
    odd = lax.rem(part_ref[0], 2)
    units, cap = h_ref.shape[1:]
    rows = hp_ref.shape[1] // FOLD
    slot_row = lax.broadcasted_iota(jnp.int32, (cap, cap), 0)
    gap = jnp.zeros((SHIFT, cap), F32)
    blank = jnp.zeros((rows - units // FOLD, cap), F32)
    for u in range(STEP):
        slot = meta_ref[u, 0:1, :].astype(jnp.int32)
        place = (slot_row == slot).astype(BF16)
        tall[...] = jnp.dot(h_ref[u], place, preferred_element_type=F32)
        out = jnp.dot(o_ref[u], place, preferred_element_type=F32)
        op_ref[u] = jnp.where(
            odd == 1, jnp.concatenate([gap, out], axis=0), jnp.concatenate([out, gap], axis=0)
        ).astype(BF16)
        for m in range(FOLD):
            picked = tall[pl.ds(m, units // FOLD, stride=FOLD), :]
            hp_ref[0, m * rows : (m + 1) * rows, u * cap : (u + 1) * cap] = jnp.concatenate(
                [picked, blank], axis=0
            ).astype(BF16)


def score_kernel(part_ref, g_ref, op_ref, s_ref, window, out, arrived):
    sources, width, _ = out.shape
    part = part_ref[0]
    start = pl.multiple_of(part * (width - SHIFT) - SHIFT * lax.rem(part, 2), 16)
    copies = []
    for i in range(sources // STEP):
        some = slice(i * STEP, (i + 1) * STEP)
        copies.append(
            (
                pltpu.make_async_copy(
                    g_ref.at[some, pl.ds(start, width), :], window.at[some], arrived.at[i, 0]
                ),
                pltpu.make_async_copy(op_ref.at[some], out.at[some], arrived.at[i, 1]),
            )
        )
    for pair in copies:
        for copy in pair:
            copy.start()
    for i, pair in enumerate(copies):
        for copy in pair:
            copy.wait()
        for u in range(i * STEP, (i + 1) * STEP):
            score = jnp.sum(out[u].astype(F32) * window[u].astype(F32), axis=0, keepdims=True)
            s_ref[u] = jnp.broadcast_to(score, s_ref.shape[1:])


def term_kernel(
    shape, meta_ref, g_ref, hp_ref, w_ref, acc, rhs, flat, grads, hidden, owned, arrived, left
):
    units, nx, nh, nl = shape
    sources, cols, cap = grads.shape
    wide = rhs.shape[0]
    copies = []
    for i in range(sources // STEP):
        copies.append([pltpu.make_async_copy(hp_ref.at[i], hidden.at[i], arrived.at[i, STEP])])
        for u in range(STEP):
            j = i * STEP + u
            copies[-1].append(pltpu.make_async_copy(g_ref.at[j], grads.at[j], arrived.at[i, u]))
    for group in copies:
        for copy in group:
            copy.start()
    rhs[cols:, :] = jnp.zeros((wide - cols, STEP * cap), BF16)
    for i, group in enumerate(copies):
        for copy in group:
            copy.wait()
        for u in range(STEP):
            j = i * STEP + u
            weight = meta_ref[j, 1:2, :]
            rhs[:cols, u * cap : (u + 1) * cap] = (grads[j].astype(F32) * weight).astype(BF16)
        for n in range(0, wide, TILE):
            term = lax.dot_general(
                hidden[i],
                rhs[n : n + TILE, :],
                (((1,), (1,)), ((), ())),
                preferred_element_type=F32,
            )
            acc[:, n : n + TILE] = term if i == 0 else acc[:, n : n + TILE] + term

    live, rows = units // FOLD, acc.shape[0] // FOLD
    span = FOLD * cols // LANE
    whole = units * cols // LANE
    flat[whole:, :] = jnp.zeros((flat.shape[0] - whole, LANE), F32)
    tail = None
    for m in range(FOLD):
        lead, offset = divmod(m * cols, LANE)
        lines = acc[m * rows : (m + 1) * rows, :]
        lines = pltpu.roll(lines, offset, 1) if offset else lines
        for t in range(wide // LANE):
            piece = lines[:live, t * LANE : (t + 1) * LANE]
            if t == 0 and offset:
                piece = piece + tail
            tail = piece
            end = (lead + t + 1) * LANE
            if end <= (m + 1) * cols:
                flat[pl.ds(lead + t, live, stride=span), :] = piece
            elif end - LANE < (m + 1) * cols:
                break
    size = owned.shape[1] // nh
    share = units * cols // (nx * nh * nl)
    lane = lax.broadcasted_iota(jnp.int32, (size, LANE), 1)
    leaving = []
    for dest in range(nx * nl):
        x, l = divmod(dest, nl)
        for h in range(nh):
            base, offset = divmod(((x * nh + h) * nl + l) * share, LANE)
            own = flat[base : base + size, :]
            if offset:
                after = flat[base + 1 : base + 1 + size, :]
                own = pltpu.roll(jnp.where(lane < offset, after, own), LANE - offset, 1)
            owned[dest, h * size : (h + 1) * size, :] = own.astype(BF16)
        leaving.append(pltpu.make_async_copy(owned.at[dest], w_ref.at[dest], left.at[dest]))
        leaving[-1].start()
    for copy in leaving:
        copy.wait()


def place(part, meta, h, o, rows):
    sources, units, cap = h.shape
    width = o.shape[1] + SHIFT
    return pl.pallas_call(
        place_kernel,
        grid_spec=pltpu.PrefetchScalarGridSpec(
            num_scalar_prefetch=1,
            grid=(sources // STEP,),
            in_specs=[
                pl.BlockSpec((STEP, 2, cap), lambda i, p: (i, 0, 0)),
                pl.BlockSpec((STEP, units, cap), lambda i, p: (i, 0, 0)),
                pl.BlockSpec((STEP, o.shape[1], cap), lambda i, p: (i, 0, 0)),
            ],
            out_specs=[
                pl.BlockSpec((1, FOLD * rows, STEP * cap), lambda i, p: (i, 0, 0)),
                pl.BlockSpec((STEP, width, cap), lambda i, p: (i, 0, 0)),
            ],
            scratch_shapes=[pltpu.VMEM((units, cap), F32)],
        ),
        out_shape=[
            jax.ShapeDtypeStruct((sources // STEP, FOLD * rows, STEP * cap), BF16),
            jax.ShapeDtypeStruct((sources, width, cap), BF16),
        ],
        compiler_params=pltpu.CompilerParams(vmem_limit_bytes=16 * 1024 * 1024),
        cost_estimate=pl.CostEstimate(
            flops=4 * sources * units * cap * cap, bytes_accessed=8 * sources * units * cap, transcendentals=0
        ),
    )(part, meta, h, o)


def scores_of(part, g, op):
    sources, width, cap = op.shape
    return pl.pallas_call(
        score_kernel,
        in_specs=[
            pl.BlockSpec(memory_space=pltpu.SMEM),
            pl.BlockSpec(memory_space=pl.ANY),
            pl.BlockSpec(memory_space=pl.ANY),
        ],
        out_shape=jax.ShapeDtypeStruct((sources, SPREAD, cap), F32),
        scratch_shapes=[
            pltpu.VMEM((sources, width, cap), BF16),
            pltpu.VMEM((sources, width, cap), BF16),
            pltpu.SemaphoreType.DMA((sources // STEP, 2)),
        ],
        compiler_params=pltpu.CompilerParams(vmem_limit_bytes=50 * 1024 * 1024),
        cost_estimate=pl.CostEstimate(
            flops=2 * sources * width * cap, bytes_accessed=4 * sources * width * cap, transcendentals=0
        ),
    )(part, g, op)


def weight_term(meta, g, hp, shape):
    units, nx, nh, nl = shape
    sources, cols, cap = g.shape
    high = hp.shape[1]
    wide = -(-cols // TILE) * TILE
    share = units * cols // (nx * nh * nl)
    size = -(-share // (16 * LANE)) * 16
    lines = -(-((nx * nh * nl - 1) * share // LANE + size + 1) // 8) * 8
    return pl.pallas_call(
        functools.partial(term_kernel, shape),
        in_specs=[
            pl.BlockSpec(memory_space=pltpu.VMEM),
            pl.BlockSpec(memory_space=pl.ANY),
            pl.BlockSpec(memory_space=pl.ANY),
        ],
        out_specs=pl.BlockSpec(memory_space=pl.ANY),
        out_shape=jax.ShapeDtypeStruct((nx * nl, nh * size, LANE), BF16),
        scratch_shapes=[
            pltpu.VMEM((high, wide), F32),
            pltpu.VMEM((wide, STEP * cap), BF16),
            pltpu.VMEM((lines, LANE), F32),
            pltpu.VMEM((sources, cols, cap), BF16),
            pltpu.VMEM(hp.shape, BF16),
            pltpu.VMEM((nx * nl, nh * size, LANE), BF16),
            pltpu.SemaphoreType.DMA((sources // STEP, STEP + 1)),
            pltpu.SemaphoreType.DMA((nx * nl,)),
        ],
        compiler_params=pltpu.CompilerParams(vmem_limit_bytes=50 * 1024 * 1024),
        cost_estimate=pl.CostEstimate(
            flops=2 * sources * cap * high * wide, bytes_accessed=2 * sources * cols * cap, transcendentals=0
        ),
    )(meta, g, hp)


def local(out_grad, routes, slots, combine_weight, saved_hidden, saved_out):
    nx, nh, nl = (lax.axis_size(name) for name in ("x", "zh", "zl"))
    blocks = lax.axis_size("y") * lax.axis_size("c")
    cap, units = saved_hidden.shape[3:]
    cols = out_grad.shape[1]
    split = cols // saved_out.shape[4]
    experts = blocks // split
    me = lax.axis_index("y") * lax.axis_size("c") + lax.axis_index("c")
    part = (me % split).reshape(1).astype(jnp.int32)
    rows = -(-(units // FOLD) // 16) * 16

    gathered = lax.all_gather(out_grad.T, ("y", "c"), axis=0)

    names = routes.T[None] == jnp.arange(experts, dtype=jnp.int32)[:, None, None]
    slot_of = jnp.sum(jnp.where(names, slots.T[None].astype(F32), 0.0), axis=1)
    weight_of = jnp.sum(jnp.where(names, combine_weight.T[None].astype(F32), 0.0), axis=1)
    sent = jnp.repeat(jnp.stack([slot_of, weight_of], axis=1), split, axis=0)
    meta = lax.all_to_all(sent, ("y", "c"), split_axis=0, concat_axis=0, tiled=True)

    h = saved_hidden[0, 0].transpose(0, 2, 1)
    o = saved_out[0, 0].transpose(0, 2, 1)
    hp, op = place(part, meta, h, o, rows)
    scores = scores_of(part, gathered, op)
    gathered, scores = lax.optimization_barrier((gathered, scores))
    everyones = lax.all_gather(scores, ("y", "c"), axis=0)
    term = weight_term(meta, gathered, hp, (units, nx, nh, nl))
    first = lax.all_to_all(term, ("x", "zl"), split_axis=0, concat_axis=0, tiled=True)
    partial_sum = jnp.sum(first.astype(F32), axis=0).astype(BF16)
    second = lax.all_to_all(
        partial_sum.reshape(nh, -1, LANE), "zh", split_axis=0, concat_axis=0, tiled=True
    )
    returned = lax.dynamic_slice_in_dim(everyones, me, 1, axis=1)[:, 0, 0]
    combined = jnp.sum(returned.reshape(experts, split, cap), axis=1)
    router_grad = jnp.sum(jnp.where(names, combined[:, None, :], 0.0), axis=0).T
    second, router_grad = lax.optimization_barrier((second, router_grad))

    summed = jnp.sum(second.astype(F32), axis=0).astype(BF16)
    weight_grad = summed.reshape(1, -1)[:, : units * cols // (nx * nh * nl)]
    return (weight_grad, router_grad)


def solution(mesh):
    nx = {64: 4, 4: 2}[mesh.shape["dp"]]
    grid = Mesh(
        mesh.devices.reshape(nx, mesh.shape["dp"] // nx // 2, 2, mesh.shape["expert"] // 2, 2),
        ("x", "zh", "zl", "y", "c"),
    )
    rows = P(("x", "zh", "zl", "y", "c"), None)
    saved = P(("x", "zh", "zl"), ("y", "c"), None, None, None)
    return jax.shard_map(
        local,
        mesh=grid,
        in_specs=(rows, rows, rows, rows, saved, saved),
        out_specs=(P(("y", "c"), ("x", "zh", "zl")), rows),
        check_vma=False,
    )
```

```python
import functools

import jax
import jax.numpy as jnp
from jax import lax
from jax.experimental import pallas as pl
from jax.experimental.pallas import tpu as pltpu
from jax.sharding import Mesh, PartitionSpec as P

F32 = jnp.float32
BF16 = jnp.bfloat16
STEP = 4
SHIFT = 8
SPREAD = 16
FOLD = 4
LANE = 128
TILE = 256
VMEM = 56 * 1024 * 1024


def place_kernel(part_ref, meta_ref, h_ref, o_ref, hp_ref, op_ref, tall):
    odd = lax.rem(part_ref[0], 2)
    units, cap = h_ref.shape[1:]
    rows = hp_ref.shape[1] // FOLD
    slot_row = lax.broadcasted_iota(jnp.int32, (cap, cap), 0)
    gap = jnp.zeros((SHIFT, cap), F32)
    blank = jnp.zeros((rows - units // FOLD, cap), F32)
    for u in range(STEP):
        slot = meta_ref[u, 0:1, :].astype(jnp.int32)
        place = (slot_row == slot).astype(BF16)
        tall[...] = jnp.dot(h_ref[u], place, preferred_element_type=F32)
        out = jnp.dot(o_ref[u], place, preferred_element_type=F32)
        op_ref[u] = jnp.where(
            odd == 1, jnp.concatenate([gap, out], axis=0), jnp.concatenate([out, gap], axis=0)
        ).astype(BF16)
        for m in range(FOLD):
            picked = tall[pl.ds(m, units // FOLD, stride=FOLD), :]
            hp_ref[0, m * rows : (m + 1) * rows, u * cap : (u + 1) * cap] = jnp.concatenate(
                [picked, blank], axis=0
            ).astype(BF16)


def term_kernel(
    shape, part_ref, meta_ref, g_ref, hp_ref, op_ref, w_ref, s_ref,
    acc, rhs, flat, grads, hidden, out, owned, arrived, left,
):
    units, nx, nh, nl = shape
    part = part_ref[0]
    width = out.shape[1]
    start = pl.multiple_of(part * (width - SHIFT) - SHIFT * lax.rem(part, 2), 16)
    sources, cols, cap = grads.shape
    wide = rhs.shape[0]
    copies = []
    for i in range(sources // STEP):
        copies.append([pltpu.make_async_copy(hp_ref.at[i], hidden.at[i], arrived.at[i, STEP])])
        for u in range(STEP):
            j = i * STEP + u
            copies[-1].append(pltpu.make_async_copy(g_ref.at[j], grads.at[j], arrived.at[i, u]))
        some = slice(i * STEP, (i + 1) * STEP)
        copies[-1].append(
            pltpu.make_async_copy(op_ref.at[some], out.at[some], arrived.at[i, STEP + 1])
        )
    for group in copies:
        for copy in group:
            copy.start()
    rhs[cols:, :] = jnp.zeros((wide - cols, STEP * cap), BF16)
    for i, group in enumerate(copies):
        for copy in group:
            copy.wait()
        for u in range(STEP):
            j = i * STEP + u
            weight = meta_ref[j, 1:2, :]
            window = grads[j, pl.ds(start, width), :].astype(F32)
            score = jnp.sum(out[j].astype(F32) * window, axis=0, keepdims=True)
            s_ref[j] = jnp.broadcast_to(score, s_ref.shape[1:])
            rhs[:cols, u * cap : (u + 1) * cap] = (grads[j].astype(F32) * weight).astype(BF16)
        for n in range(0, wide, TILE):
            term = lax.dot_general(
                hidden[i],
                rhs[n : n + TILE, :],
                (((1,), (1,)), ((), ())),
                preferred_element_type=F32,
            )
            acc[:, n : n + TILE] = term if i == 0 else acc[:, n : n + TILE] + term

    live, rows = units // FOLD, acc.shape[0] // FOLD
    span = FOLD * cols // LANE
    whole = units * cols // LANE
    flat[whole:, :] = jnp.zeros((flat.shape[0] - whole, LANE), F32)
    tail = None
    for m in range(FOLD):
        lead, offset = divmod(m * cols, LANE)
        lines = acc[m * rows : (m + 1) * rows, :]
        lines = pltpu.roll(lines, offset, 1) if offset else lines
        for t in range(wide // LANE):
            piece = lines[:live, t * LANE : (t + 1) * LANE]
            if t == 0 and offset:
                piece = piece + tail
            tail = piece
            end = (lead + t + 1) * LANE
            if end <= (m + 1) * cols:
                flat[pl.ds(lead + t, live, stride=span), :] = piece
            elif end - LANE < (m + 1) * cols:
                break
    size = owned.shape[1] // nh
    share = units * cols // (nx * nh * nl)
    lane = lax.broadcasted_iota(jnp.int32, (size, LANE), 1)
    leaving = []
    for dest in range(nx * nl):
        x, l = divmod(dest, nl)
        for h in range(nh):
            base, offset = divmod(((x * nh + h) * nl + l) * share, LANE)
            own = flat[base : base + size, :]
            if offset:
                after = flat[base + 1 : base + 1 + size, :]
                own = pltpu.roll(jnp.where(lane < offset, after, own), LANE - offset, 1)
            owned[dest, h * size : (h + 1) * size, :] = own.astype(BF16)
        leaving.append(pltpu.make_async_copy(owned.at[dest], w_ref.at[dest], left.at[dest]))
        leaving[-1].start()
    for copy in leaving:
        copy.wait()


def place(part, meta, h, o, rows):
    sources, units, cap = h.shape
    width = o.shape[1] + SHIFT
    return pl.pallas_call(
        place_kernel,
        grid_spec=pltpu.PrefetchScalarGridSpec(
            num_scalar_prefetch=1,
            grid=(sources // STEP,),
            in_specs=[
                pl.BlockSpec((STEP, 2, cap), lambda i, p: (i, 0, 0)),
                pl.BlockSpec((STEP, units, cap), lambda i, p: (i, 0, 0)),
                pl.BlockSpec((STEP, o.shape[1], cap), lambda i, p: (i, 0, 0)),
            ],
            out_specs=[
                pl.BlockSpec((1, FOLD * rows, STEP * cap), lambda i, p: (i, 0, 0)),
                pl.BlockSpec((STEP, width, cap), lambda i, p: (i, 0, 0)),
            ],
            scratch_shapes=[pltpu.VMEM((units, cap), F32)],
        ),
        out_shape=[
            jax.ShapeDtypeStruct((sources // STEP, FOLD * rows, STEP * cap), BF16),
            jax.ShapeDtypeStruct((sources, width, cap), BF16),
        ],
        compiler_params=pltpu.CompilerParams(vmem_limit_bytes=16 * 1024 * 1024),
        cost_estimate=pl.CostEstimate(
            flops=4 * sources * units * cap * cap, bytes_accessed=8 * sources * units * cap, transcendentals=0
        ),
    )(part, meta, h, o)


def weight_term(part, meta, g, hp, op, shape):
    units, nx, nh, nl = shape
    sources, cols, cap = g.shape
    high = hp.shape[1]
    wide = -(-cols // TILE) * TILE
    share = units * cols // (nx * nh * nl)
    size = -(-share // (16 * LANE)) * 16
    lines = -(-((nx * nh * nl - 1) * share // LANE + size + 1) // 8) * 8
    return pl.pallas_call(
        functools.partial(term_kernel, shape),
        in_specs=[
            pl.BlockSpec(memory_space=pltpu.SMEM),
            pl.BlockSpec(memory_space=pltpu.VMEM),
            pl.BlockSpec(memory_space=pl.ANY),
            pl.BlockSpec(memory_space=pl.ANY),
            pl.BlockSpec(memory_space=pl.ANY),
        ],
        out_specs=[
            pl.BlockSpec(memory_space=pl.ANY),
            pl.BlockSpec(memory_space=pltpu.VMEM),
        ],
        out_shape=[
            jax.ShapeDtypeStruct((nx * nl, nh * size, LANE), BF16),
            jax.ShapeDtypeStruct((sources, SPREAD, cap), F32),
        ],
        scratch_shapes=[
            pltpu.VMEM((high, wide), F32),
            pltpu.VMEM((wide, STEP * cap), BF16),
            pltpu.VMEM((lines, LANE), F32),
            pltpu.VMEM((sources, cols, cap), BF16),
            pltpu.VMEM(hp.shape, BF16),
            pltpu.VMEM(op.shape, BF16),
            pltpu.VMEM((nx * nl, nh * size, LANE), BF16),
            pltpu.SemaphoreType.DMA((sources // STEP, STEP + 2)),
            pltpu.SemaphoreType.DMA((nx * nl,)),
        ],
        compiler_params=pltpu.CompilerParams(vmem_limit_bytes=46 * 1024 * 1024),
        cost_estimate=pl.CostEstimate(
            flops=2 * sources * cap * high * wide, bytes_accessed=2 * sources * cols * cap, transcendentals=0
        ),
    )(part, meta, g, hp, op)


def local(out_grad, routes, slots, combine_weight, saved_hidden, saved_out):
    nx, nh, nl = (lax.axis_size(name) for name in ("x", "zh", "zl"))
    blocks = lax.axis_size("y") * lax.axis_size("c")
    cap, units = saved_hidden.shape[3:]
    cols = out_grad.shape[1]
    split = cols // saved_out.shape[4]
    experts = blocks // split
    me = lax.axis_index("y") * lax.axis_size("c") + lax.axis_index("c")
    part = (me % split).reshape(1).astype(jnp.int32)
    rows = -(-(units // FOLD) // 16) * 16

    gathered = lax.all_gather(out_grad.T, ("y", "c"), axis=0)

    names = routes.T[None] == jnp.arange(experts, dtype=jnp.int32)[:, None, None]
    slot_of = jnp.sum(jnp.where(names, slots.T[None].astype(F32), 0.0), axis=1)
    weight_of = jnp.sum(jnp.where(names, combine_weight.T[None].astype(F32), 0.0), axis=1)
    sent = jnp.repeat(jnp.stack([slot_of, weight_of], axis=1), split, axis=0)
    meta = lax.all_to_all(sent, ("y", "c"), split_axis=0, concat_axis=0, tiled=True)

    h = saved_hidden[0, 0].transpose(0, 2, 1)
    o = saved_out[0, 0].transpose(0, 2, 1)
    hp, op = place(part, meta, h, o, rows)
    term, scores = weight_term(part, meta, gathered, hp, op, (units, nx, nh, nl))
    everyones = lax.all_gather(scores, ("y", "c"), axis=0)

    first = lax.all_to_all(term, ("x", "zl"), split_axis=0, concat_axis=0, tiled=True)
    partial_sum = jnp.sum(first.astype(F32), axis=0).astype(BF16)
    second = lax.all_to_all(
        partial_sum.reshape(nh, -1, LANE), "zh", split_axis=0, concat_axis=0, tiled=True
    )
    returned = lax.dynamic_slice_in_dim(everyones, me, 1, axis=1)[:, 0, 0]
    combined = jnp.sum(returned.reshape(experts, split, cap), axis=1)
    router_grad = jnp.sum(jnp.where(names, combined[:, None, :], 0.0), axis=0).T
    second, router_grad = lax.optimization_barrier((second, router_grad))

    summed = jnp.sum(second.astype(F32), axis=0).astype(BF16)
    weight_grad = summed.reshape(1, -1)[:, : units * cols // (nx * nh * nl)]
    return (weight_grad, router_grad)


def solution(mesh):
    nx = {64: 4, 4: 2}[mesh.shape["dp"]]
    grid = Mesh(
        mesh.devices.reshape(nx, mesh.shape["dp"] // nx // 2, 2, mesh.shape["expert"] // 2, 2),
        ("x", "zh", "zl", "y", "c"),
    )
    rows = P(("x", "zh", "zl", "y", "c"), None)
    saved = P(("x", "zh", "zl"), ("y", "c"), None, None, None)
    return jax.shard_map(
        local,
        mesh=grid,
        in_specs=(rows, rows, rows, rows, saved, saved),
        out_specs=(P(("y", "c"), ("x", "zh", "zl")), rows),
        check_vma=False,
    )
```

```python
import functools

import jax
import jax.numpy as jnp
from jax import lax
from jax.experimental import pallas as pl
from jax.experimental.pallas import tpu as pltpu
from jax.sharding import Mesh, PartitionSpec as P

F32 = jnp.float32
BF16 = jnp.bfloat16
STEP = 4
SHIFT = 8
SPREAD = 16
FOLD = 4
LANE = 128
TILE = 256
VMEM = 56 * 1024 * 1024


def place_kernel(part_ref, meta_ref, h_ref, o_ref, hp_ref, op_ref, tall):
    odd = lax.rem(part_ref[0], 2)
    units, cap = h_ref.shape[1:]
    rows = hp_ref.shape[1] // FOLD
    slot_row = lax.broadcasted_iota(jnp.int32, (cap, cap), 0)
    gap = jnp.zeros((SHIFT, cap), F32)
    blank = jnp.zeros((rows - units // FOLD, cap), F32)
    for u in range(STEP):
        slot = meta_ref[u, 0:1, :].astype(jnp.int32)
        place = (slot_row == slot).astype(BF16)
        tall[...] = jnp.dot(h_ref[u], place, preferred_element_type=F32)
        out = jnp.dot(o_ref[u], place, preferred_element_type=F32)
        op_ref[u] = jnp.where(
            odd == 1, jnp.concatenate([gap, out], axis=0), jnp.concatenate([out, gap], axis=0)
        ).astype(BF16)
        for m in range(FOLD):
            picked = tall[pl.ds(m, units // FOLD, stride=FOLD), :]
            hp_ref[0, m * rows : (m + 1) * rows, u * cap : (u + 1) * cap] = jnp.concatenate(
                [picked, blank], axis=0
            ).astype(BF16)


def term_kernel(
    shape, part_ref, meta_ref, g_ref, hp_ref, op_ref, w_ref, s_ref,
    acc, rhs, flat, grads, hidden, out, owned, arrived, left,
):
    units, nx, nh, nl = shape
    part = part_ref[0]
    width = out.shape[1]
    start = pl.multiple_of(part * (width - SHIFT) - SHIFT * lax.rem(part, 2), 16)
    sources, cols, cap = grads.shape
    wide = rhs.shape[0]
    copies = []
    for i in range(sources // STEP):
        copies.append([pltpu.make_async_copy(hp_ref.at[i], hidden.at[i], arrived.at[i, STEP])])
        for u in range(STEP):
            j = i * STEP + u
            copies[-1].append(pltpu.make_async_copy(g_ref.at[j], grads.at[j], arrived.at[i, u]))
        some = slice(i * STEP, (i + 1) * STEP)
        copies[-1].append(
            pltpu.make_async_copy(op_ref.at[some], out.at[some], arrived.at[i, STEP + 1])
        )
    for group in copies:
        for copy in group:
            copy.start()
    rhs[cols:, :] = jnp.zeros((wide - cols, STEP * cap), BF16)
    for i, group in enumerate(copies):
        for copy in group:
            copy.wait()
        for u in range(STEP):
            j = i * STEP + u
            weight = meta_ref[j, 1:2, :]
            window = grads[j, pl.ds(start, width), :].astype(F32)
            score = jnp.sum(out[j].astype(F32) * window, axis=0, keepdims=True)
            s_ref[j] = jnp.broadcast_to(score, s_ref.shape[1:])
            rhs[:cols, u * cap : (u + 1) * cap] = grads[j] * weight.astype(BF16)
        for n in range(0, wide, TILE):
            term = lax.dot_general(
                hidden[i],
                rhs[n : n + TILE, :],
                (((1,), (1,)), ((), ())),
                preferred_element_type=F32,
            )
            acc[:, n : n + TILE] = term if i == 0 else acc[:, n : n + TILE] + term

    live, rows = units // FOLD, acc.shape[0] // FOLD
    span = FOLD * cols // LANE
    whole = units * cols // LANE
    flat[whole:, :] = jnp.zeros((flat.shape[0] - whole, LANE), F32)
    tail = None
    for m in range(FOLD):
        lead, offset = divmod(m * cols, LANE)
        lines = acc[m * rows : (m + 1) * rows, :]
        lines = pltpu.roll(lines, offset, 1) if offset else lines
        for t in range(wide // LANE):
            piece = lines[:live, t * LANE : (t + 1) * LANE]
            if t == 0 and offset:
                piece = piece + tail
            tail = piece
            end = (lead + t + 1) * LANE
            if end <= (m + 1) * cols:
                flat[pl.ds(lead + t, live, stride=span), :] = piece
            elif end - LANE < (m + 1) * cols:
                break
    size = owned.shape[1] // nh
    share = units * cols // (nx * nh * nl)
    lane = lax.broadcasted_iota(jnp.int32, (size, LANE), 1)
    leaving = []
    for dest in range(nx * nl):
        x, l = divmod(dest, nl)
        for h in range(nh):
            base, offset = divmod(((x * nh + h) * nl + l) * share, LANE)
            own = flat[base : base + size, :]
            if offset:
                after = flat[base + 1 : base + 1 + size, :]
                own = pltpu.roll(jnp.where(lane < offset, after, own), LANE - offset, 1)
            owned[dest, h * size : (h + 1) * size, :] = own.astype(BF16)
        leaving.append(pltpu.make_async_copy(owned.at[dest], w_ref.at[dest], left.at[dest]))
        leaving[-1].start()
    for copy in leaving:
        copy.wait()


def place(part, meta, h, o, rows):
    sources, units, cap = h.shape
    width = o.shape[1] + SHIFT
    return pl.pallas_call(
        place_kernel,
        grid_spec=pltpu.PrefetchScalarGridSpec(
            num_scalar_prefetch=1,
            grid=(sources // STEP,),
            in_specs=[
                pl.BlockSpec((STEP, 2, cap), lambda i, p: (i, 0, 0)),
                pl.BlockSpec((STEP, units, cap), lambda i, p: (i, 0, 0)),
                pl.BlockSpec((STEP, o.shape[1], cap), lambda i, p: (i, 0, 0)),
            ],
            out_specs=[
                pl.BlockSpec((1, FOLD * rows, STEP * cap), lambda i, p: (i, 0, 0)),
                pl.BlockSpec((STEP, width, cap), lambda i, p: (i, 0, 0)),
            ],
            scratch_shapes=[pltpu.VMEM((units, cap), F32)],
        ),
        out_shape=[
            jax.ShapeDtypeStruct((sources // STEP, FOLD * rows, STEP * cap), BF16),
            jax.ShapeDtypeStruct((sources, width, cap), BF16),
        ],
        compiler_params=pltpu.CompilerParams(vmem_limit_bytes=VMEM),
        cost_estimate=pl.CostEstimate(
            flops=4 * sources * units * cap * cap, bytes_accessed=8 * sources * units * cap, transcendentals=0
        ),
    )(part, meta, h, o)


def weight_term(part, meta, g, hp, op, shape):
    units, nx, nh, nl = shape
    sources, cols, cap = g.shape
    high = hp.shape[1]
    wide = -(-cols // TILE) * TILE
    share = units * cols // (nx * nh * nl)
    size = -(-share // (16 * LANE)) * 16
    lines = -(-((nx * nh * nl - 1) * share // LANE + size + 1) // 8) * 8
    return pl.pallas_call(
        functools.partial(term_kernel, shape),
        in_specs=[
            pl.BlockSpec(memory_space=pltpu.SMEM),
            pl.BlockSpec(memory_space=pltpu.VMEM),
            pl.BlockSpec(memory_space=pl.ANY),
            pl.BlockSpec(memory_space=pl.ANY),
            pl.BlockSpec(memory_space=pl.ANY),
        ],
        out_specs=[
            pl.BlockSpec(memory_space=pl.ANY),
            pl.BlockSpec(memory_space=pltpu.VMEM),
        ],
        out_shape=[
            jax.ShapeDtypeStruct((nx * nl, nh * size, LANE), BF16),
            jax.ShapeDtypeStruct((sources, SPREAD, cap), F32),
        ],
        scratch_shapes=[
            pltpu.VMEM((high, wide), F32),
            pltpu.VMEM((wide, STEP * cap), BF16),
            pltpu.VMEM((lines, LANE), F32),
            pltpu.VMEM((sources, cols, cap), BF16),
            pltpu.VMEM(hp.shape, BF16),
            pltpu.VMEM(op.shape, BF16),
            pltpu.VMEM((nx * nl, nh * size, LANE), BF16),
            pltpu.SemaphoreType.DMA((sources // STEP, STEP + 2)),
            pltpu.SemaphoreType.DMA((nx * nl,)),
        ],
        compiler_params=pltpu.CompilerParams(vmem_limit_bytes=VMEM),
        cost_estimate=pl.CostEstimate(
            flops=2 * sources * cap * high * wide, bytes_accessed=2 * sources * cols * cap, transcendentals=0
        ),
    )(part, meta, g, hp, op)


def local(out_grad, routes, slots, combine_weight, saved_hidden, saved_out):
    nx, nh, nl = (lax.axis_size(name) for name in ("x", "zh", "zl"))
    blocks = lax.axis_size("y") * lax.axis_size("c")
    cap, units = saved_hidden.shape[3:]
    cols = out_grad.shape[1]
    split = cols // saved_out.shape[4]
    experts = blocks // split
    me = lax.axis_index("y") * lax.axis_size("c") + lax.axis_index("c")
    part = (me % split).reshape(1).astype(jnp.int32)
    rows = -(-(units // FOLD) // 16) * 16

    gathered = lax.all_gather(out_grad.T, ("y", "c"), axis=0)

    names = routes.T[None] == jnp.arange(experts, dtype=jnp.int32)[:, None, None]
    slot_of = jnp.sum(jnp.where(names, slots.T[None].astype(F32), 0.0), axis=1)
    weight_of = jnp.sum(jnp.where(names, combine_weight.T[None].astype(F32), 0.0), axis=1)
    sent = jnp.repeat(jnp.stack([slot_of, weight_of], axis=1), split, axis=0)
    meta = lax.all_to_all(sent, ("y", "c"), split_axis=0, concat_axis=0, tiled=True)

    h = saved_hidden[0, 0].transpose(0, 2, 1)
    o = saved_out[0, 0].transpose(0, 2, 1)
    hp, op = place(part, meta, h, o, rows)
    term, scores = weight_term(part, meta, gathered, hp, op, (units, nx, nh, nl))
    everyones = lax.all_gather(scores, ("y", "c"), axis=0)

    first = lax.all_to_all(term, ("x", "zl"), split_axis=0, concat_axis=0, tiled=True)
    partial_sum = jnp.sum(first.astype(F32), axis=0).astype(BF16)
    second = lax.all_to_all(
        partial_sum.reshape(nh, -1, LANE), "zh", split_axis=0, concat_axis=0, tiled=True
    )
    returned = lax.dynamic_slice_in_dim(everyones, me, 1, axis=1)[:, 0, 0]
    combined = jnp.sum(returned.reshape(experts, split, cap), axis=1)
    router_grad = jnp.sum(jnp.where(names, combined[:, None, :], 0.0), axis=0).T
    second, router_grad = lax.optimization_barrier((second, router_grad))

    summed = jnp.sum(second.astype(F32), axis=0).astype(BF16)
    weight_grad = summed.reshape(1, -1)[:, : units * cols // (nx * nh * nl)]
    return (weight_grad, router_grad)


def solution(mesh):
    nx = {64: 4, 4: 2}[mesh.shape["dp"]]
    grid = Mesh(
        mesh.devices.reshape(nx, mesh.shape["dp"] // nx // 2, 2, mesh.shape["expert"] // 2, 2),
        ("x", "zh", "zl", "y", "c"),
    )
    rows = P(("x", "zh", "zl", "y", "c"), None)
    saved = P(("x", "zh", "zl"), ("y", "c"), None, None, None)
    return jax.shard_map(
        local,
        mesh=grid,
        in_specs=(rows, rows, rows, rows, saved, saved),
        out_specs=(P(("y", "c"), ("x", "zh", "zl")), rows),
        check_vma=False,
    )
```
